32 devices in a mesh: pipe: 4 (over z), ctx: 2 (over y), dp: 4 (over x, core).
Axes of the slice: x: 2, y: 2, z: 4, core: 2. Of those that a mesh axis runs over, the one named last changes fastest.
Arguments:
- queries: bfloat16 [4, 4, 256, 4096], P('pipe', 'dp', 'ctx'), may hold values from -7 to 7
- key_input: bfloat16 [4, 4, 256, 512], P('pipe', 'dp', 'ctx'), may hold values from -4 to 4
- value_input: bfloat16 [4, 4, 256, 512], P('pipe', 'dp', 'ctx'), may hold values from -6 to 6
- incoming: bfloat16 [4, 4, 256, 4096], P('pipe', 'dp', 'ctx'), may hold values from -6 to 6
- segments: int32 [4, 256], P('dp'), may hold values from 0 to 3, never falling along the last dimension, each value on 1 to 128 neighbouring positions
Outputs:
- query_grad: bfloat16 [4, 4, 256, 4096], P('pipe', 'dp', 'ctx')
- key_grad: bfloat16 [4, 4, 256, 512], P('pipe', 'dp', 'ctx')
- value_grad: bfloat16 [4, 4, 256, 512], P('pipe', 'dp', 'ctx')
- bias_grad: float32 [4, 5120], P('pipe')
The draws below stay inside these ranges and needn't reach their ends.
Inputs may be any that keep to these rules, and one draw needn't show every extreme that they name: `segments`: tokens of one document are contiguous; every document holds 1 to 128 tokens and one holds exactly 128.
All inputs are finite; a program needn't handle non-finite values.
Results may differ from the reference program's by a relative error of at most 0.009.
Values may be sent and summed in bfloat16 or wider, within the bound.
A program may use at most 64 MiB of HBM per device.

```python
import math
import jax
import jax.numpy as jnp
import numpy as np
from jax import lax

ASKER_STREAMS = 32
SHARED_GROUPS = 4
FEATURE_SIZE = 128
QUERY_PER_KEY = 8
DOC_MOST = 128
LOT_POSITIONS = 256
DOCS = 4
RELAY_PHASES = 4
SMALL_LOTS = 4


def draw_queries(key, part):
    array_dims = (RELAY_PHASES, SMALL_LOTS, LOT_POSITIONS, ASKER_STREAMS, FEATURE_SIZE)
    noise = jnp.clip(jax.random.normal(jax.random.fold_in(key, 11), array_dims, jnp.float32), -4.0, 4.0)
    value_tensor = noise
    return value_tensor.reshape(RELAY_PHASES, SMALL_LOTS, LOT_POSITIONS, ASKER_STREAMS * FEATURE_SIZE).astype(jnp.bfloat16)


def draw_key_input(key, part):
    array_dims = (RELAY_PHASES, SMALL_LOTS, LOT_POSITIONS, SHARED_GROUPS, FEATURE_SIZE)
    noise = jnp.clip(jax.random.normal(jax.random.fold_in(key, 21), array_dims, jnp.float32), -4.0, 4.0)
    value_tensor = noise
    return value_tensor.reshape(RELAY_PHASES, SMALL_LOTS, LOT_POSITIONS, SHARED_GROUPS * FEATURE_SIZE).astype(jnp.bfloat16)


def level_of(stream_key, shape, shards, least, high):
    gain = 1.0
    for axis_at, shards_of in shards:
        steps = jax.random.uniform(jax.random.fold_in(jax.random.fold_in(stream_key, 6), axis_at), (shards_of,), jnp.float32, least / len(shards), high / len(shards))
        gain = gain * jnp.repeat(jnp.exp(steps), shape[axis_at] // shards_of).reshape((-1,) + (1,) * (len(shape) - 1 - axis_at))
    return gain


def profile(number_of, total, limit, lean):
    weights = [(1 << 20) // math.isqrt(grade ** lean) + 1 for grade in range(2, number_of + 1)]
    spare, counts = total - limit - (number_of - 1), [1] * (number_of - 1)
    while spare > 0:
        candidates = [i for i in range(number_of - 1) if counts[i] < limit]
        pool, remaining = sum([weights[i] for i in candidates]), spare
        for i in candidates:
            addition = min(limit - counts[i], max(1, remaining * weights[i] // pool), spare)
            counts[i] = counts[i] + addition
            spare = spare - addition
    return np.array([limit] + counts)


def uneven_parts(stream_key, amount, total, most, skew):
    if amount == 2:
        one = jax.random.randint(stream_key, (), max(1, total - most), min(most, total - 1) + 1)
        return jnp.stack([one, total - one])
    lengths = jnp.asarray(profile(amount, total, most, skew), jnp.int32)
    twos = (amount - 1) // 2
    source_of, taker = lengths[1:1 + 2 * twos:2], lengths[2:2 + 2 * twos:2]
    room = jnp.minimum(source_of - 1, most - taker)
    shifted = jax.random.randint(jax.random.fold_in(stream_key, 1), (twos,), 0, 1 << 20) % (room + 1)
    lengths = lengths.at[1:1 + 2 * twos:2].set(source_of - shifted).at[2:2 + 2 * twos:2].set(taker + shifted)
    return lengths[jax.random.permutation(jax.random.fold_in(stream_key, 2), amount)]


def scatter_about(own_key, extent, scale, limit, split=(), kind=jnp.bfloat16):
    array = scale * jax.random.normal(own_key, extent, jnp.float32)
    if split:
        array = array * level_of(own_key, extent, split, -0.22, 0.18)
    return jnp.clip(array, -limit, limit).astype(kind)


def setup_inputs(seed: int = 0) -> dict:
    key_of = jax.random.split(jax.random.key(seed), 6)
    queries = draw_queries(jax.random.fold_in(key_of[5], 71), 0)
    key_input = draw_key_input(jax.random.fold_in(key_of[5], 71), 0)
    value_input = scatter_about(key_of[2], (RELAY_PHASES, SMALL_LOTS, LOT_POSITIONS, SHARED_GROUPS * FEATURE_SIZE), 1.0, 6.0, ((0, 4), (1, 4), (2, 2)))
    incoming = scatter_about(key_of[3], (RELAY_PHASES, SMALL_LOTS, LOT_POSITIONS, ASKER_STREAMS * FEATURE_SIZE), 1.0, 6.0, ((0, 4), (1, 4), (2, 2)))
    segments = jax.vmap(lambda own: jnp.searchsorted(jnp.cumsum(uneven_parts(own, DOCS, LOT_POSITIONS, DOC_MOST, 1)), jnp.arange(LOT_POSITIONS), side="right"))(jax.random.split(key_of[4], SMALL_LOTS)).reshape((SMALL_LOTS, LOT_POSITIONS)).astype(jnp.int32)
    return {"queries": queries, "key_input": key_input, "value_input": value_input, "incoming": incoming, "segments": segments}


def attend(queries, key_rows, value_rows, cotangent, query_doc, key_doc, query_pos, key_pos, scaling):
    queries = queries.astype(jnp.float32)
    key_rows = key_rows.astype(jnp.float32)
    value_rows = value_rows.astype(jnp.float32)
    cotangent = cotangent.astype(jnp.float32)
    scores = jnp.einsum('gqd,kd->gqk', queries, key_rows) * scaling
    visible = (query_doc[:, None] == key_doc[None, :]) & (key_pos[None, :] <= query_pos[:, None])
    scores = jnp.where(visible[None], scores, -1e+30)
    row_max = lax.optimization_barrier(jnp.max(scores, axis=-1, keepdims=True))
    weights = jnp.where(visible[None], jnp.exp(scores - row_max), 0.0)
    probs = weights / lax.optimization_barrier(jnp.sum(weights, axis=-1, keepdims=True))
    probs_b = lax.optimization_barrier(probs.astype(jnp.bfloat16)).astype(jnp.float32)
    attn_out = jnp.einsum('gqk,kd->gqd', probs_b, value_rows)
    dot_out = lax.optimization_barrier(jnp.sum(cotangent * attn_out, axis=-1, keepdims=True))
    grad_prob = jnp.einsum('gqd,kd->gqk', cotangent, value_rows)
    grad_score = (probs * (grad_prob - dot_out) * scaling).astype(jnp.bfloat16)
    grad_score = lax.optimization_barrier(grad_score).astype(jnp.float32)
    asker_derivative = jnp.einsum('gqk,kd->gqd', grad_score, key_rows)
    lookup_derivative = jnp.einsum('gqk,gqd->kd', grad_score, queries)
    content_derivative = jnp.einsum('gqk,gqd->kd', probs_b, cotangent)
    return (asker_derivative, lookup_derivative, content_derivative)

def banded(queries, key_rows, value_rows, cotangent, doc_ids, block_len, scaling):
    length = doc_ids.shape[0]
    blocks = length // block_len
    width = key_rows.shape[1]
    key_pad = jnp.concatenate([jnp.zeros((block_len, width), key_rows.dtype), key_rows], axis=0)
    value_pad = jnp.concatenate([jnp.zeros((block_len, width), value_rows.dtype), value_rows], axis=0)
    doc_pad = jnp.concatenate([jnp.full((block_len,), -1, jnp.int32), doc_ids.astype(jnp.int32)])
    pos_pad = jnp.arange(length + block_len, dtype=jnp.int32) - block_len

    def step(carried, block):
        key_acc, value_acc = carried
        anchor = (block * block_len).astype(jnp.int32)
        query_blk = lax.dynamic_slice_in_dim(queries, anchor, block_len, 1)
        cot_blk = lax.dynamic_slice_in_dim(cotangent, anchor, block_len, 1)
        key_blk = lax.dynamic_slice_in_dim(key_pad, anchor, 2 * block_len, 0)
        value_blk = lax.dynamic_slice_in_dim(value_pad, anchor, 2 * block_len, 0)
        query_doc = lax.dynamic_slice_in_dim(doc_ids.astype(jnp.int32), anchor, block_len, 0)
        key_doc = lax.dynamic_slice_in_dim(doc_pad, anchor, 2 * block_len, 0)
        query_pos = anchor + jnp.arange(block_len, dtype=jnp.int32)
        key_pos = lax.dynamic_slice_in_dim(pos_pad, anchor, 2 * block_len, 0)
        asker_derivative, lookup_derivative, content_derivative = attend(query_blk, key_blk, value_blk, cot_blk, query_doc, key_doc, query_pos, key_pos, scaling)
        key_acc = lax.dynamic_update_slice_in_dim(key_acc, lax.dynamic_slice_in_dim(key_acc, anchor, 2 * block_len, 0) + lookup_derivative, anchor, 0)
        value_acc = lax.dynamic_update_slice_in_dim(value_acc, lax.dynamic_slice_in_dim(value_acc, anchor, 2 * block_len, 0) + content_derivative, anchor, 0)
        return ((key_acc, value_acc), asker_derivative)
    start_acc = jnp.zeros((length + block_len, width), jnp.float32)
    (key_acc, value_acc), query_blocks = lax.scan(step, (start_acc, start_acc), jnp.arange(blocks, dtype=jnp.int32))
    groups = queries.shape[0]
    asker_derivative = query_blocks.transpose(1, 0, 2, 3).reshape(groups, length, width)
    return (asker_derivative, key_acc[block_len:], value_acc[block_len:])

def reference(queries, key_input, value_input, incoming, segments):
    scaling = 1.0 / math.sqrt(FEATURE_SIZE)
    grad_q_all, grad_k_all, grad_v_all, offset_entire = ([], [], [], [])
    for phase_index in range(RELAY_PHASES):
        phase_q, phase_k, phase_v = ([], [], [])
        offset_parts = jnp.zeros(((ASKER_STREAMS + 2 * SHARED_GROUPS) * FEATURE_SIZE,), jnp.float32)
        for micro_batch_index in range(SMALL_LOTS):
            query_per_head = queries[phase_index, micro_batch_index].reshape(LOT_POSITIONS, SHARED_GROUPS, QUERY_PER_KEY, FEATURE_SIZE).transpose(1, 2, 0, 3)
            output_grad_heads = incoming[(phase_index + 1) % RELAY_PHASES, micro_batch_index].reshape(LOT_POSITIONS, SHARED_GROUPS, QUERY_PER_KEY, FEATURE_SIZE).transpose(1, 2, 0, 3)
            key_per_head = key_input[phase_index, micro_batch_index].reshape(LOT_POSITIONS, SHARED_GROUPS, FEATURE_SIZE).transpose(1, 0, 2)
            value_per_head = value_input[phase_index, micro_batch_index].reshape(LOT_POSITIONS, SHARED_GROUPS, FEATURE_SIZE).transpose(1, 0, 2)
            doc_ids = segments[micro_batch_index]

            def per_head(members):
                return banded(members[0], members[1], members[2], members[3], doc_ids, DOC_MOST, scaling)
            asker_derivative, lookup_derivative, content_derivative = lax.map(per_head, (query_per_head, key_per_head, value_per_head, output_grad_heads))
            asker_derivative = asker_derivative.transpose(2, 0, 1, 3).reshape(LOT_POSITIONS, ASKER_STREAMS * FEATURE_SIZE)
            lookup_derivative = lookup_derivative.transpose(1, 0, 2).reshape(LOT_POSITIONS, SHARED_GROUPS * FEATURE_SIZE)
            content_derivative = content_derivative.transpose(1, 0, 2).reshape(LOT_POSITIONS, SHARED_GROUPS * FEATURE_SIZE)
            offset_parts = offset_parts + jnp.concatenate([lax.optimization_barrier(jnp.sum(asker_derivative, axis=0)), lax.optimization_barrier(jnp.sum(lookup_derivative, axis=0)), lax.optimization_barrier(jnp.sum(content_derivative, axis=0))])
            phase_q.append(asker_derivative.astype(jnp.bfloat16))
            phase_k.append(lookup_derivative.astype(jnp.bfloat16))
            phase_v.append(content_derivative.astype(jnp.bfloat16))
        grad_q_all.append(jnp.stack(phase_q))
        grad_k_all.append(jnp.stack(phase_k))
        grad_v_all.append(jnp.stack(phase_v))
        offset_entire.append(offset_parts / math.sqrt(SMALL_LOTS * LOT_POSITIONS))
    return (jnp.stack(grad_q_all), jnp.stack(grad_k_all), jnp.stack(grad_v_all), jnp.stack(offset_entire))
```

```python
import functools
import math

import jax
import jax.numpy as jnp
from jax import lax
from jax.experimental import pallas as pl
from jax.experimental.pallas import tpu as pltpu
from jax.sharding import PartitionSpec as P

ASKER_STREAMS = 32
SHARED_GROUPS = 4
FEATURE_SIZE = 128
QUERY_PER_KEY = 8
HALF = 4
BIAS_ROWS = 16
MESH = pl.DeviceIdType.MESH
F32 = jnp.float32
BF16 = jnp.bfloat16


def dot(a, b, a_dim, b_dim):
    return lax.dot_general(a, b, (((a_dim,), (b_dim,)), ((), ())), preferred_element_type=F32)


def kernel(
    sizes, in_kernel_sum,
    q_hbm, k_hbm, v_hbm, inc_hbm, seg_hbm,
    dq_hbm, dk_hbm, dv_hbm, bias_hbm,
    q_rows, cot_rows, keys, values, seg, mask_add, probs, acc, dq_rows,
    back_out, back_in, bias_mine, bias_in, dk_out, dv_out, bias_out,
    q_sem, cot_send, cot_recv, own_sem, halo_send, halo_recv, seg_sem,
    back_send, back_recv, bias_send, bias_recv, dq_sem, out_sem,
):
    pipe, ctx, dp, reach = sizes
    rows = q_hbm.shape[0]
    width = FEATURE_SIZE
    window = (reach + 1) * rows
    length = seg_hbm.shape[1]
    scaling = 1.0 / math.sqrt(FEATURE_SIZE)
    my_pipe, my_ctx, my_dp = lax.axis_index("pipe"), lax.axis_index("ctx"), lax.axis_index("dp")

    below = lax.rem(my_pipe + pipe - 1, pipe)
    above = lax.rem(my_pipe + 1, pipe)
    offsets = [(d, c) for d in range(dp) for c in range(ctx) if (d, c) != (0, 0)]

    def peer(d, c):
        return {"dp": lax.rem(my_dp + d, dp), "ctx": lax.rem(my_ctx + c, ctx)}

    def ahead(r):
        return {"ctx": lax.rem(my_ctx + r, ctx)}

    def behind(r):
        return {"ctx": lax.rem(my_ctx + ctx - r, ctx)}

    def columns(index):
        return pl.ds(pl.multiple_of(index * width, width), width)

    def head_rows(index):
        return pl.ds(pl.multiple_of(index * rows, rows), rows)

    def cot_copy(h):
        return pltpu.make_async_remote_copy(
            src_ref=inc_hbm.at[:, columns(h)], dst_ref=cot_rows.at[head_rows(h)],
            send_sem=cot_send.at[h], recv_sem=cot_recv.at[h],
            device_id={"pipe": below}, device_id_type=MESH,
        )

    def q_copy(h):
        return pltpu.make_async_copy(q_hbm.at[:, columns(h)], q_rows.at[head_rows(h)], q_sem.at[h])

    def dq_copy(h):
        return pltpu.make_async_copy(dq_rows.at[head_rows(h)], dq_hbm.at[:, columns(h)], dq_sem.at[h])

    def halo_copy(i, r):
        src, dst = (k_hbm, keys) if i == 0 else (v_hbm, values)
        return pltpu.make_async_remote_copy(
            src_ref=src, dst_ref=dst.at[pl.ds((reach - r) * rows, rows)],
            send_sem=halo_send.at[i, r - 1], recv_sem=halo_recv.at[i, r - 1],
            device_id=ahead(r), device_id_type=MESH,
        )

    def back_copy(g, r):
        return pltpu.make_async_remote_copy(
            src_ref=back_out.at[g, r - 1], dst_ref=back_in.at[g, r - 1],
            send_sem=back_send.at[g, r - 1], recv_sem=back_recv.at[g, r - 1],
            device_id=behind(r), device_id_type=MESH,
        )

    def bias_copy(g, i):
        return pltpu.make_async_remote_copy(
            src_ref=bias_mine.at[g], dst_ref=bias_in.at[i, g],
            send_sem=bias_send.at[i, g], recv_sem=bias_recv.at[i, g],
            device_id=peer(*offsets[i]), device_id_type=MESH,
        )

    own_copies = [
        pltpu.make_async_copy(k_hbm, keys.at[pl.ds(reach * rows, rows)], own_sem.at[0]),
        pltpu.make_async_copy(v_hbm, values.at[pl.ds(reach * rows, rows)], own_sem.at[1]),
    ]
    seg_copy = pltpu.make_async_copy(seg_hbm, seg, seg_sem)

    barrier = pltpu.get_barrier_semaphore()
    greeted = [{"pipe": below}, {"pipe": above}]
    if in_kernel_sum:
        greeted += [peer(d, c) for d, c in offsets]
    else:
        greeted += [ahead(r) for r in range(1, reach + 1)] + [behind(r) for r in range(1, reach + 1)]
    for other in greeted:
        pl.semaphore_signal(barrier, inc=1, device_id=other, device_id_type=MESH)
    seg_copy.start()
    for copy in own_copies:
        copy.start()

    @pl.loop(0, ASKER_STREAMS)
    def _(h):
        q_copy(h).start()

    pl.semaphore_wait(barrier, len(greeted))

    for r in range(1, reach + 1):
        for i in range(2):
            halo_copy(i, r).start()

    @pl.loop(0, ASKER_STREAMS)
    def _(h):
        cot_copy(h).start()

    seg_copy.wait()
    query_doc = seg[:, pl.ds(pl.multiple_of(my_ctx * rows, rows), rows)].astype(F32)
    query_pos = lax.broadcasted_iota(jnp.int32, (rows, rows), 1) + my_ctx * rows
    for b in range(reach + 1):
        r = reach - b
        block = lax.rem(my_ctx + ctx - r, ctx)
        key_doc = seg[:, pl.ds(pl.multiple_of(block * rows, rows), rows)].astype(F32)
        key_doc = jnp.broadcast_to(key_doc, (rows, rows)).T
        key_pos = lax.broadcasted_iota(jnp.int32, (rows, rows), 0) + (my_ctx - r) * rows
        visible = (key_doc == query_doc) & (key_pos <= query_pos) & (key_pos >= 0)
        mask_add[pl.ds(b * rows, rows), :] = jnp.where(visible, 0.0, -1e30)

    @pl.loop(0, ASKER_STREAMS)
    def _(h):
        q_copy(h).wait()

    for copy in own_copies:
        copy.wait()
    for r in range(1, reach + 1):
        for i in range(2):
            halo_copy(i, r).wait_recv()

    to_exp2 = scaling * math.log2(math.e)

    @pl.loop(0, SHARED_GROUPS)
    def _(g):
        key_block = keys[:, columns(g)]
        for i in range(QUERY_PER_KEY):
            h = g * QUERY_PER_KEY + i
            scores = dot(key_block, q_rows[head_rows(h), :], 1, 1) * to_exp2 + mask_add[...]
            weights = jnp.exp2(scores - jnp.max(scores, axis=0, keepdims=True))
            probs[h] = weights * (1.0 / jnp.sum(weights, axis=0, keepdims=True))

    @pl.loop(0, SHARED_GROUPS)
    def _(g):
        key_block = keys[:, columns(g)]
        value_block = values[:, columns(g)]
        for half in range(QUERY_PER_KEY // HALF):
            first = g * QUERY_PER_KEY + half * HALF
            grads, probs_b = [], []
            for i in range(HALF):
                h = first + i
                cot_copy(h).wait_recv()
                p = probs[h]
                pb = p.astype(BF16)
                grad_prob = dot(value_block, cot_rows[head_rows(h), :], 1, 1)
                dot_out = jnp.sum(pb.astype(F32) * grad_prob, axis=0, keepdims=True)
                grads.append((p * (grad_prob - dot_out) * scaling).astype(BF16))
                probs_b.append(pb)
            grads = jnp.concatenate(grads, axis=1)
            probs_b = jnp.concatenate(probs_b, axis=1)
            these = pl.ds(pl.multiple_of(first * rows, rows), HALF * rows)
            dk = dot(grads, q_rows[these, :], 1, 0)
            dv = dot(probs_b, cot_rows[these, :], 1, 0)
            if half:
                dk = acc[g, 0] + dk
                dv = acc[g, 1] + dv
            acc[g, 0] = dk
            acc[g, 1] = dv
            if half == QUERY_PER_KEY // HALF - 1:
                for r in range(1, reach + 1):
                    part = slice((reach - r) * rows, (reach - r + 1) * rows)
                    back_out[g, r - 1, 0] = dk[part].astype(BF16)
                    back_out[g, r - 1, 1] = dv[part].astype(BF16)
                    back_copy(g, r).start()
                bias_mine[g, 8:9, :] = jnp.sum(dk, axis=0, keepdims=True)
                bias_mine[g, 9:10, :] = jnp.sum(dv, axis=0, keepdims=True)
            dq = dot(grads, key_block, 0, 0)
            dq_rows[these, :] = dq.astype(BF16)
            for i in range(HALF):
                row = half * HALF + i
                bias_mine[g, row : row + 1, :] = jnp.sum(
                    dq[i * rows : (i + 1) * rows], axis=0, keepdims=True
                )
                dq_copy(first + i).start()
        if in_kernel_sum:
            for i in range(len(offsets)):
                bias_copy(g, i).start()

    for g in range(SHARED_GROUPS):
        part = pl.ds(g * width, width)
        dk = acc[g, 0, pl.ds(reach * rows, rows), :]
        dv = acc[g, 1, pl.ds(reach * rows, rows), :]
        for r in range(1, reach + 1):
            back_copy(g, r).wait_recv()
            dk = dk + back_in[g, r - 1, 0].astype(F32)
            dv = dv + back_in[g, r - 1, 1].astype(F32)
        dk_out[:, part] = dk.astype(BF16)
        dv_out[:, part] = dv.astype(BF16)
    outs = [
        pltpu.make_async_copy(dk_out, dk_hbm, out_sem.at[0]),
        pltpu.make_async_copy(dv_out, dv_hbm, out_sem.at[1]),
        pltpu.make_async_copy(bias_out, bias_hbm, out_sem.at[2]),
    ]
    outs[0].start()
    outs[1].start()

    bias_scale = 1.0 / math.sqrt(dp * length)
    for g in range(SHARED_GROUPS):
        total = bias_mine[g]
        if in_kernel_sum:
            for i in range(len(offsets)):
                bias_copy(g, i).wait_recv()
                total = total + bias_in[i, g]
        total = total * bias_scale
        for i in range(QUERY_PER_KEY):
            bias_out[:, pl.ds((g * QUERY_PER_KEY + i) * width, width)] = total[i : i + 1, :]
        bias_out[:, pl.ds((ASKER_STREAMS + g) * width, width)] = total[8:9, :]
        bias_out[:, pl.ds((ASKER_STREAMS + SHARED_GROUPS + g) * width, width)] = total[9:10, :]
    outs[2].start()

    for r in range(1, reach + 1):
        for i in range(2):
            halo_copy(i, r).wait_send()
        for g in range(SHARED_GROUPS):
            back_copy(g, r).wait_send()
    if in_kernel_sum:
        for i in range(len(offsets)):
            for g in range(SHARED_GROUPS):
                bias_copy(g, i).wait_send()

    @pl.loop(0, ASKER_STREAMS)
    def _(h):
        cot_copy(h).wait_send()
        dq_copy(h).wait()

    for copy in outs:
        copy.wait()


def body(pipe, ctx, dp, queries, key_input, value_input, incoming, segments):
    rows = queries.shape[2]
    length = segments.shape[1]
    reach = min(4, ctx - 1)
    window = (reach + 1) * rows
    in_kernel_sum = dp * ctx <= 16
    peers = dp * ctx - 1 if in_kernel_sum else 1
    q_width = ASKER_STREAMS * FEATURE_SIZE
    kv_width = SHARED_GROUPS * FEATURE_SIZE
    dma = pltpu.SemaphoreType.DMA
    dq, dk, dv, bias = pl.pallas_call(
        functools.partial(kernel, (pipe, ctx, dp, reach), in_kernel_sum),
        out_shape=(
            jax.ShapeDtypeStruct((rows, q_width), BF16),
            jax.ShapeDtypeStruct((rows, kv_width), BF16),
            jax.ShapeDtypeStruct((rows, kv_width), BF16),
            jax.ShapeDtypeStruct((1, q_width + 2 * kv_width), F32),
        ),
        in_specs=[pl.BlockSpec(memory_space=pl.ANY)] * 5,
        out_specs=[pl.BlockSpec(memory_space=pl.ANY)] * 4,
        scratch_shapes=[
            pltpu.VMEM((ASKER_STREAMS * rows, FEATURE_SIZE), BF16),
            pltpu.VMEM((ASKER_STREAMS * rows, FEATURE_SIZE), BF16),
            pltpu.VMEM((window, kv_width), BF16),
            pltpu.VMEM((window, kv_width), BF16),
            pltpu.VMEM((1, length), jnp.int32),
            pltpu.VMEM((window, rows), F32),
            pltpu.VMEM((ASKER_STREAMS, window, rows), F32),
            pltpu.VMEM((SHARED_GROUPS, 2, window, FEATURE_SIZE), F32),
            pltpu.VMEM((ASKER_STREAMS * rows, FEATURE_SIZE), BF16),
            pltpu.VMEM((SHARED_GROUPS, reach, 2, rows, FEATURE_SIZE), BF16),
            pltpu.VMEM((SHARED_GROUPS, reach, 2, rows, FEATURE_SIZE), BF16),
            pltpu.VMEM((SHARED_GROUPS, BIAS_ROWS, FEATURE_SIZE), F32),
            pltpu.VMEM((peers, SHARED_GROUPS, BIAS_ROWS, FEATURE_SIZE), F32),
            pltpu.VMEM((rows, kv_width), BF16),
            pltpu.VMEM((rows, kv_width), BF16),
            pltpu.VMEM((1, q_width + 2 * kv_width), F32),
            dma((ASKER_STREAMS,)),
            dma((ASKER_STREAMS,)),
            dma((ASKER_STREAMS,)),
            dma((2,)),
            dma((2, reach)),
            dma((2, reach)),
            dma,
            dma((SHARED_GROUPS, reach)),
            dma((SHARED_GROUPS, reach)),
            dma((peers, SHARED_GROUPS)),
            dma((peers, SHARED_GROUPS)),
            dma((ASKER_STREAMS,)),
            dma((3,)),
        ],
        compiler_params=pltpu.CompilerParams(
            collective_id=0, has_side_effects=True, vmem_limit_bytes=48 * 1024 * 1024
        ),
    )(queries[0, 0], key_input[0, 0], value_input[0, 0], incoming[0, 0], segments)
    if not in_kernel_sum:
        bias = lax.psum(bias, ("ctx", "dp"))
    return dq[None, None], dk[None, None], dv[None, None], bias


def solution(mesh):
    tokens = P("pipe", "dp", "ctx", None)
    return jax.shard_map(
        functools.partial(body, mesh.shape["pipe"], mesh.shape["ctx"], mesh.shape["dp"]),
        mesh=mesh,
        in_specs=(tokens, tokens, tokens, tokens, P("dp", None)),
        out_specs=(tokens, tokens, tokens, P("pipe", None)),
        check_vma=False,
    )
```

```python
import functools
import math

import jax
import jax.numpy as jnp
from jax import lax
from jax.experimental import pallas as pl
from jax.experimental.pallas import tpu as pltpu
from jax.sharding import PartitionSpec as P

ASKER_STREAMS = 32
SHARED_GROUPS = 4
FEATURE_SIZE = 128
QUERY_PER_KEY = 8
PAIR = 2
BIAS_ROWS = 16
MESH = pl.DeviceIdType.MESH
F32 = jnp.float32
BF16 = jnp.bfloat16
VMEM_GRANT = 62 * 1024 * 1024


def dot(a, b, a_dim, b_dim):
    return lax.dot_general(a, b, (((a_dim,), (b_dim,)), ((), ())), preferred_element_type=F32)


def kernel(
    sizes, in_kernel_sum,
    q_hbm, k_hbm, v_hbm, inc_hbm, seg_hbm,
    dq_hbm, dk_hbm, dv_hbm, bias_hbm,
    q_rows, cot_rows, keys, values, seg, mask_add, probs, acc, dq_rows,
    back_out, back_in, bias_mine, bias_in, dk_out, dv_out, bias_out,
    q_sem, cot_send, cot_recv, own_sem, halo_send, halo_recv, seg_sem,
    back_send, back_recv, bias_send, bias_recv, dq_sem, out_sem,
):
    pipe, ctx, dp, reach = sizes
    rows = q_hbm.shape[0]
    width = FEATURE_SIZE
    window = (reach + 1) * rows
    length = seg_hbm.shape[1]
    scaling = 1.0 / math.sqrt(FEATURE_SIZE)
    my_pipe, my_ctx, my_dp = lax.axis_index("pipe"), lax.axis_index("ctx"), lax.axis_index("dp")

    below = lax.rem(my_pipe + pipe - 1, pipe)
    above = lax.rem(my_pipe + 1, pipe)
    offsets = [(d, c) for d in range(dp) for c in range(ctx) if (d, c) != (0, 0)]

    def peer(d, c):
        return {"dp": lax.rem(my_dp + d, dp), "ctx": lax.rem(my_ctx + c, ctx)}

    def ahead(r):
        return {"ctx": lax.rem(my_ctx + r, ctx)}

    def behind(r):
        return {"ctx": lax.rem(my_ctx + ctx - r, ctx)}

    def columns(index):
        return pl.ds(pl.multiple_of(index * width, width), width)

    def head_rows(index):
        return pl.ds(pl.multiple_of(index * rows, rows), rows)

    def cot_copy(h):
        return pltpu.make_async_remote_copy(
            src_ref=inc_hbm.at[:, columns(h)], dst_ref=cot_rows.at[head_rows(h)],
            send_sem=cot_send.at[h], recv_sem=cot_recv.at[h],
            device_id={"pipe": below}, device_id_type=MESH,
        )

    def q_copy(h):
        return pltpu.make_async_copy(q_hbm.at[:, columns(h)], q_rows.at[head_rows(h)], q_sem.at[h])

    def dq_copy(h):
        return pltpu.make_async_copy(dq_rows.at[head_rows(h)], dq_hbm.at[:, columns(h)], dq_sem.at[h])

    def halo_copy(i, r):
        src, dst = (k_hbm, keys) if i == 0 else (v_hbm, values)
        return pltpu.make_async_remote_copy(
            src_ref=src, dst_ref=dst.at[pl.ds((reach - r) * rows, rows)],
            send_sem=halo_send.at[i, r - 1], recv_sem=halo_recv.at[i, r - 1],
            device_id=ahead(r), device_id_type=MESH,
        )

    def back_copy(g, r, i):
        return pltpu.make_async_remote_copy(
            src_ref=back_out.at[g, r - 1, i], dst_ref=back_in.at[g, r - 1, i],
            send_sem=back_send.at[g, r - 1, i], recv_sem=back_recv.at[g, r - 1, i],
            device_id=behind(r), device_id_type=MESH,
        )

    def bias_copy(g, i):
        return pltpu.make_async_remote_copy(
            src_ref=bias_mine.at[g], dst_ref=bias_in.at[i, g],
            send_sem=bias_send.at[i, g], recv_sem=bias_recv.at[i, g],
            device_id=peer(*offsets[i]), device_id_type=MESH,
        )

    own_copies = [
        pltpu.make_async_copy(k_hbm, keys.at[pl.ds(reach * rows, rows)], own_sem.at[0]),
        pltpu.make_async_copy(v_hbm, values.at[pl.ds(reach * rows, rows)], own_sem.at[1]),
    ]
    seg_copy = pltpu.make_async_copy(seg_hbm, seg, seg_sem)

    barrier = pltpu.get_barrier_semaphore()
    greeted = [{"pipe": below}, {"pipe": above}]
    if in_kernel_sum:
        greeted += [peer(d, c) for d, c in offsets]
    else:
        greeted += [ahead(r) for r in range(1, reach + 1)] + [behind(r) for r in range(1, reach + 1)]
    for other in greeted:
        pl.semaphore_signal(barrier, inc=1, device_id=other, device_id_type=MESH)
    seg_copy.start()
    for copy in own_copies:
        copy.start()

    @pl.loop(0, ASKER_STREAMS)
    def _(h):
        q_copy(h).start()

    pl.semaphore_wait(barrier, len(greeted))

    @pl.loop(0, ASKER_STREAMS)
    def _(h):
        cot_copy(h).start()

    for r in range(1, reach + 1):
        for i in range(2):
            halo_copy(i, r).start()

    seg_copy.wait()
    query_doc = seg[:, pl.ds(pl.multiple_of(my_ctx * rows, rows), rows)].astype(F32)
    query_pos = lax.broadcasted_iota(jnp.int32, (rows, rows), 1) + my_ctx * rows
    for b in range(reach + 1):
        r = reach - b
        block = lax.rem(my_ctx + ctx - r, ctx)
        key_doc = seg[:, pl.ds(pl.multiple_of(block * rows, rows), rows)].astype(F32)
        key_doc = jnp.broadcast_to(key_doc, (rows, rows)).T
        key_pos = lax.broadcasted_iota(jnp.int32, (rows, rows), 0) + (my_ctx - r) * rows
        visible = (key_doc == query_doc) & (key_pos <= query_pos) & (key_pos >= 0)
        mask_add[pl.ds(b * rows, rows), :] = jnp.where(visible, 0.0, -1e30)

    @pl.loop(0, ASKER_STREAMS)
    def _(h):
        q_copy(h).wait()

    for copy in own_copies:
        copy.wait()
    for r in range(1, reach + 1):
        for i in range(2):
            halo_copy(i, r).wait_recv()

    to_exp2 = scaling * math.log2(math.e)

    @pl.loop(0, SHARED_GROUPS)
    def _(g):
        key_block = keys[:, columns(g)]
        for i in range(QUERY_PER_KEY):
            h = g * QUERY_PER_KEY + i
            scores = dot(key_block, q_rows[head_rows(h), :], 1, 1) * to_exp2 + mask_add[...]
            weights = jnp.exp2(scores - jnp.max(scores, axis=0, keepdims=True))
            probs[h] = weights * (1.0 / jnp.sum(weights, axis=0, keepdims=True))

    def send_back(g, i, grad):
        for r in range(1, reach + 1):
            part = slice((reach - r) * rows, (reach - r + 1) * rows)
            back_out[g, r - 1, i] = grad[part].astype(BF16)
            back_copy(g, r, i).start()

    def wait_sent(g):
        for i in range(QUERY_PER_KEY):
            cot_copy(g * QUERY_PER_KEY + i).wait_send()
            dq_copy(g * QUERY_PER_KEY + i).wait()
        for r in range(1, reach + 1):
            for i in range(2):
                back_copy(g, r, i).wait_send()
        if in_kernel_sum:
            for i in range(len(offsets)):
                bias_copy(g, i).wait_send()

    @pl.loop(0, SHARED_GROUPS)
    def _(g):
        key_block = keys[:, columns(g)]
        value_block = values[:, columns(g)]
        for pair in range(QUERY_PER_KEY // PAIR):
            last = pair == QUERY_PER_KEY // PAIR - 1
            first = g * QUERY_PER_KEY + pair * PAIR
            these = pl.ds(pl.multiple_of(first * rows, rows), PAIR * rows)
            grads = []
            for i in range(PAIR):
                h = first + i
                cot_copy(h).wait_recv()
                if i == PAIR - 1:
                    probs_b = jnp.concatenate(
                        [probs[first + n].astype(BF16) for n in range(PAIR)], axis=1
                    )
                    dv = dot(probs_b, cot_rows[these, :], 1, 0)
                    if pair:
                        dv = acc[g, 1] + dv
                    acc[g, 1] = dv
                    if last:
                        send_back(g, 1, dv)
                p = probs[h]
                grad_prob = dot(value_block, cot_rows[head_rows(h), :], 1, 1)
                dot_out = jnp.sum(p.astype(BF16).astype(F32) * grad_prob, axis=0, keepdims=True)
                grads.append((p * (grad_prob - dot_out) * scaling).astype(BF16))
            grads = jnp.concatenate(grads, axis=1)
            dk = dot(grads, q_rows[these, :], 1, 0)
            if pair:
                dk = acc[g, 0] + dk
            acc[g, 0] = dk
            if last:
                send_back(g, 0, dk)
            dq = dot(grads, key_block, 0, 0)
            for i in range(PAIR):
                row = pair * PAIR + i
                bias_mine[g, row : row + 1, :] = jnp.sum(
                    dq[i * rows : (i + 1) * rows], axis=0, keepdims=True
                )
            if last:
                bias_mine[g, 8:9, :] = jnp.sum(dk, axis=0, keepdims=True)
                bias_mine[g, 9:10, :] = jnp.sum(dv, axis=0, keepdims=True)
                if in_kernel_sum:
                    for i in range(len(offsets)):
                        bias_copy(g, i).start()
            dq_rows[these, :] = dq.astype(BF16)
            for i in range(PAIR):
                dq_copy(first + i).start()

        @pl.when(g > 0)
        def _():
            wait_sent(g - 1)

    bias_scale = 1.0 / math.sqrt(dp * length)

    def finish_bias(g):
        total = bias_mine[g]
        if in_kernel_sum:
            for i in range(len(offsets)):
                bias_copy(g, i).wait_recv()
                total = total + bias_in[i, g]
        total = total * bias_scale
        for i in range(QUERY_PER_KEY):
            bias_out[:, pl.ds((g * QUERY_PER_KEY + i) * width, width)] = total[i : i + 1, :]
        bias_out[:, pl.ds((ASKER_STREAMS + g) * width, width)] = total[8:9, :]
        bias_out[:, pl.ds((ASKER_STREAMS + SHARED_GROUPS + g) * width, width)] = total[9:10, :]

    def finish_kv(g, i, out):
        total = acc[g, i, pl.ds(reach * rows, rows), :]
        for r in range(1, reach + 1):
            back_copy(g, r, i).wait_recv()
            total = total + back_in[g, r - 1, i].astype(F32)
        out[:, pl.ds(g * width, width)] = total.astype(BF16)

    outs = [
        pltpu.make_async_copy(dk_out, dk_hbm, out_sem.at[0]),
        pltpu.make_async_copy(dv_out, dv_hbm, out_sem.at[1]),
        pltpu.make_async_copy(bias_out, bias_hbm, out_sem.at[2]),
    ]
    for g in range(SHARED_GROUPS):
        finish_kv(g, 1, dv_out)
        if g < SHARED_GROUPS - 1:
            finish_bias(g)
            finish_kv(g, 0, dk_out)
    outs[1].start()
    finish_kv(SHARED_GROUPS - 1, 0, dk_out)
    outs[0].start()
    finish_bias(SHARED_GROUPS - 1)
    outs[2].start()

    for r in range(1, reach + 1):
        for i in range(2):
            halo_copy(i, r).wait_send()
    wait_sent(SHARED_GROUPS - 1)
    for copy in outs:
        copy.wait()


def write_out(*refs):
    count = len(refs) // 3
    ins, outs, held = refs[:count], refs[count : 2 * count], refs[2 * count : 3 * count]
    in_sem, out_sem = refs[3 * count :]
    parts = [(0, pl.ds(n * 32, 32)) for n in range(ins[0].shape[0] // 32)]
    parts += [(i, slice(None)) for i in range(1, count)]

    def copy(n, source, target, sem):
        i, part = parts[n]
        return pltpu.make_async_copy(source[i].at[part], target[i].at[part], sem.at[n])

    for n in range(len(parts)):
        copy(n, ins, held, in_sem).start()
    for n in range(len(parts)):
        copy(n, ins, held, in_sem).wait()
        copy(n, held, outs, out_sem).start()
    for n in range(len(parts)):
        copy(n, held, outs, out_sem).wait()


def body(pipe, ctx, dp, queries, key_input, value_input, incoming, segments):
    rows = queries.shape[2]
    length = segments.shape[1]
    reach = min(4, ctx - 1)
    window = (reach + 1) * rows
    in_kernel_sum = dp * ctx <= 16
    peers = dp * ctx - 1 if in_kernel_sum else 1
    q_width = ASKER_STREAMS * FEATURE_SIZE
    kv_width = SHARED_GROUPS * FEATURE_SIZE
    dma = pltpu.SemaphoreType.DMA
    shapes = (
        jax.ShapeDtypeStruct((rows, q_width), BF16),
        jax.ShapeDtypeStruct((rows, kv_width), BF16),
        jax.ShapeDtypeStruct((rows, kv_width), BF16),
        jax.ShapeDtypeStruct((1, q_width + 2 * kv_width), F32),
    )
    results = pl.pallas_call(
        functools.partial(kernel, (pipe, ctx, dp, reach), in_kernel_sum),
        out_shape=shapes,
        in_specs=[pl.BlockSpec(memory_space=pl.ANY)] * 5,
        out_specs=[pl.BlockSpec(memory_space=pl.ANY)] * 4,
        scratch_shapes=[
            pltpu.VMEM((ASKER_STREAMS * rows, FEATURE_SIZE), BF16),
            pltpu.VMEM((ASKER_STREAMS * rows, FEATURE_SIZE), BF16),
            pltpu.VMEM((window, kv_width), BF16),
            pltpu.VMEM((window, kv_width), BF16),
            pltpu.VMEM((1, length), jnp.int32),
            pltpu.VMEM((window, rows), F32),
            pltpu.VMEM((ASKER_STREAMS, window, rows), F32),
            pltpu.VMEM((SHARED_GROUPS, 2, window, FEATURE_SIZE), F32),
            pltpu.VMEM((ASKER_STREAMS * rows, FEATURE_SIZE), BF16),
            pltpu.VMEM((SHARED_GROUPS, reach, 2, rows, FEATURE_SIZE), BF16),
            pltpu.VMEM((SHARED_GROUPS, reach, 2, rows, FEATURE_SIZE), BF16),
            pltpu.VMEM((SHARED_GROUPS, BIAS_ROWS, FEATURE_SIZE), F32),
            pltpu.VMEM((peers, SHARED_GROUPS, BIAS_ROWS, FEATURE_SIZE), F32),
            pltpu.VMEM((rows, kv_width), BF16),
            pltpu.VMEM((rows, kv_width), BF16),
            pltpu.VMEM((1, q_width + 2 * kv_width), F32),
            dma((ASKER_STREAMS,)),
            dma((ASKER_STREAMS,)),
            dma((ASKER_STREAMS,)),
            dma((2,)),
            dma((2, reach)),
            dma((2, reach)),
            dma,
            dma((SHARED_GROUPS, reach, 2)),
            dma((SHARED_GROUPS, reach, 2)),
            dma((peers, SHARED_GROUPS)),
            dma((peers, SHARED_GROUPS)),
            dma((ASKER_STREAMS,)),
            dma((3,)),
        ],
        compiler_params=pltpu.CompilerParams(
            collective_id=0, has_side_effects=True, vmem_limit_bytes=VMEM_GRANT
        ),
    )(queries[0, 0], key_input[0, 0], value_input[0, 0], incoming[0, 0], segments)
    dq, dk, dv, bias = pl.pallas_call(
        write_out,
        out_shape=shapes,
        in_specs=[pl.BlockSpec(memory_space=pl.ANY)] * 4,
        out_specs=[pl.BlockSpec(memory_space=pl.ANY)] * 4,
        scratch_shapes=[pltpu.VMEM(shape.shape, shape.dtype) for shape in shapes]
        + [dma((rows // 32 + 3,)), dma((rows // 32 + 3,))],
    )(*results)
    if not in_kernel_sum:
        bias = lax.psum(bias, ("ctx", "dp"))
    return dq[None, None], dk[None, None], dv[None, None], bias


def solution(mesh):
    tokens = P("pipe", "dp", "ctx", None)
    return jax.shard_map(
        functools.partial(body, mesh.shape["pipe"], mesh.shape["ctx"], mesh.shape["dp"]),
        mesh=mesh,
        in_specs=(tokens, tokens, tokens, tokens, P("dp", None)),
        out_specs=(tokens, tokens, tokens, P("pipe", None)),
        check_vma=False,
    )
```
